32 devices in a mesh: img: 4 (over y, core), cin: 2 (over x), cout: 4 (over z).
Axes of the slice: x: 2, y: 2, z: 4, core: 2. Of those that a mesh axis runs over, the one named last changes fastest.
Arguments:
- maps: bfloat16 [2, 4, 14, 14, 1024], P(None, 'img'), may hold values from -6 to 6
- w_first: bfloat16 [3, 3, 1024, 1024], P(None, None, 'cin', 'cout'), may hold values from -0.09375 to 0.09375
- w_reduce: bfloat16 [3, 3, 1024, 8192], P(None, None, 'img', ('cin', 'cout')), may hold values from -0.09375 to 0.09375
- w_wide: bfloat16 [3, 3, 8192, 8192], P(None, None, 'cin', ('img', 'cout')), may hold values from -0.03125 to 0.03125
Outputs:
- wide_out: bfloat16 [2, 4, 7, 7, 8192], P(None, 'cin', None, None, ('img', 'cout'))
The draws below stay inside these ranges and needn't reach their ends.
All inputs are finite; a program needn't handle non-finite values.
Results may differ from the reference program's by a relative error of at most 0.014.
Values may be sent and summed in bfloat16 or wider, within the bound.
A program may use at most 128 MiB of HBM per device.

```python
import jax
import jax.numpy as jnp

C1 = 1024
C2 = 8192
MAP = 14
MB = 2
HALF = 7
IMAGES = 4


def level_of(stream_key, shape, shards, least, top_value):
    def one(dim, shards_of):
        heights = jax.random.uniform(jax.random.fold_in(jax.random.fold_in(stream_key, 6), dim), (shards_of,), jnp.float32, least / len(shards), top_value / len(shards))
        return jnp.repeat(jnp.exp(heights), shape[dim] // shards_of).reshape((-1,) + (1,) * (len(shape) - dim - 1))

    level = one(*shards[0])
    for cut in shards[1:]:
        level = level * one(*cut)
    return level


def centred(own_key, dims, width, reach, split=(), kind=jnp.bfloat16):
    level = level_of(own_key, dims, split, -0.22, 0.18) if split else 1.0
    drawn = jax.random.normal(own_key, dims, jnp.float32) * width * level
    return jnp.minimum(jnp.maximum(drawn, -reach), reach).astype(kind)


def setup_inputs(seed: int = 0) -> dict:
    splits = jax.random.split(jax.random.key(seed), 5)
    return {
        "maps": centred(splits[0], (MB, IMAGES, MAP, MAP, C1), 1.0, 6.0, ((1, 4),)),
        "w_first": centred(splits[1], (3, 3, C1, C1), (9 * C1 // 2) ** -0.5, 0.09375, ((2, 2), (3, 4))),
        "w_reduce": centred(splits[2], (3, 3, C1, C2), (9 * C1 // 2) ** -0.5, 0.09375, ((2, 4), (3, 8))),
        "w_wide": centred(splits[3], (3, 3, C2, C2), (9 * C2 // 2) ** -0.5, 0.03125, ((2, 2), (3, 16))),
    }


def conv_taps(padded, weight, size, step):
    channels = padded.shape[3]
    windows = []
    for row_tap in range(3):
        for col_tap in range(3):
            windows.append(padded[:, row_tap:row_tap + step * (size - 1) + 1:step, col_tap:col_tap + step * (size - 1) + 1:step, :])
    table = jnp.concatenate(windows, axis=3).reshape(-1, 9 * channels)
    total = jnp.dot(table, weight.reshape(9 * channels, weight.shape[3]), preferred_element_type=jnp.float32)
    return total.reshape(padded.shape[0], size, size, weight.shape[3])


def pad_map(values):
    return jnp.pad(values, ((0, 0), (1, 1), (1, 1), (0, 0)))


def reference(maps, w_first, w_reduce, w_wide):
    flat = maps.reshape(MB * IMAGES, MAP, MAP, C1)
    rectified = jnp.maximum(flat, 0)
    segment_maps = (flat.astype(jnp.float32) + conv_taps(pad_map(rectified), w_first, MAP, 1)).astype(jnp.bfloat16)
    reduced = conv_taps(pad_map(jnp.maximum(segment_maps, 0)), w_reduce, HALF, 2)
    narrow = jnp.maximum(reduced, 0.0).astype(jnp.bfloat16)
    wide_out = conv_taps(pad_map(narrow), w_wide, HALF, 1).astype(jnp.bfloat16)
    return wide_out.reshape(MB, IMAGES, HALF, HALF, C2)
```

```python
import functools

import jax
import jax.numpy as jnp
from jax import lax
from jax.experimental import pallas as pl
from jax.experimental.pallas import tpu as pltpu
from jax.sharding import PartitionSpec as P

MESH = pl.DeviceIdType.MESH
F32 = jnp.float32
BF16 = jnp.bfloat16


def by_distance(position, count, rank):
    value = 0
    for place in range(count):
        order = sorted(range(count), key=lambda other: (abs(other - place), other))
        value = value + jnp.where(position == place, order[rank], 0)
    return value


def segment_kernel(
    dims,
    maps,
    w_first,
    w_reduce,
    w_wide,
    out,
    wf,
    wr,
    ww,
    xin,
    resid,
    xpad,
    x3,
    t1,
    res16,
    p1s,
    p1r,
    line,
    segr,
    s2,
    x9,
    p2,
    cs,
    rc,
    ys,
    ry,
    nar,
    npad,
    total,
    fs,
    fr,
    load_sem,
    ww_sem,
    p1_sem,
    line_send,
    line_recv,
    seg_recv,
    core_send,
    core_recv,
    y_sem,
    nar_send,
    nar_recv,
    f_sem,
):
    zn = dims["cout"]
    side, half = dims["side"], dims["half"]
    me_i, me_x, me_z = lax.axis_index("img"), lax.axis_index("cin"), lax.axis_index("cout")
    core, me_y = lax.rem(me_i, 2), me_i // 2
    core_peer = me_y * 2 + (1 - core)
    y_peer = (1 - me_y) * 2 + core
    cb = wf.shape[2]
    ob = wf.shape[3]
    q16 = x3.shape[3]
    rows1 = side * q16
    kb = nar.shape[2]
    npos = half * half
    rows = npos * 8

    def remote(src, dst, send, recv, img, cin, cout):
        return pltpu.make_async_remote_copy(
            src_ref=src,
            dst_ref=dst,
            send_sem=send,
            recv_sem=recv,
            device_id=(img, cin, cout),
            device_id_type=MESH,
        )

    load_wf = pltpu.make_async_copy(w_first, wf, load_sem.at[0])
    load_x = pltpu.make_async_copy(
        maps.at[:, 0, :, :, pl.ds(pl.multiple_of(me_x * cb, cb), cb)], xin, load_sem.at[1]
    )
    load_r = pltpu.make_async_copy(
        maps.at[me_x, 0, :, :, pl.ds(pl.multiple_of(me_z * ob, ob), ob)], resid, load_sem.at[2]
    )
    load_wr = pltpu.make_async_copy(w_reduce, wr, load_sem.at[3])
    load_x.start()
    load_wf.start()
    load_r.start()
    load_wr.start()

    def load_ww(chunk):
        return pltpu.make_async_copy(
            w_wide.at[:, :, pl.ds(pl.multiple_of(chunk * kb, kb), kb), :], ww.at[chunk], ww_sem.at[chunk]
        )

    @pl.loop(0, ww.shape[0])
    def _(chunk):
        load_ww(chunk).start()

    barrier = pltpu.get_barrier_semaphore()
    for di in range(4):
        for dx in range(2):
            if di or dx:
                pl.semaphore_signal(
                    barrier,
                    inc=1,
                    device_id=(lax.rem(me_i + di, 4), lax.rem(me_x + dx, 2), me_z),
                    device_id_type=MESH,
                )

    @pl.when(me_z > 0)
    def _():
        pl.semaphore_signal(barrier, inc=1, device_id=(me_i, me_x, me_z - 1), device_id_type=MESH)

    @pl.when(me_z < zn - 1)
    def _():
        pl.semaphore_signal(barrier, inc=1, device_id=(me_i, me_x, me_z + 1), device_id_type=MESH)

    xpad[...] = jnp.zeros_like(xpad)
    x3[...] = jnp.zeros_like(x3)
    res16[...] = jnp.zeros_like(res16)
    s2[...] = jnp.zeros_like(s2)
    npad[...] = jnp.zeros_like(npad)
    total[...] = jnp.zeros_like(total)
    load_x.wait()
    for m in range(2):
        xpad[:, 8 : 8 + side, :] = jnp.maximum(xin[m].astype(F32), 0.0)
        for b in range(3):
            x3[b, m, 1 : 1 + side] = xpad[:, 7 + b : 7 + b + q16, :].astype(BF16)
    load_r.wait()
    res16[:, 0:side, :] = resid[...].astype(F32)
    load_wf.wait()

    @pl.loop(0, 2)
    def _(turn):
        m = jnp.where(turn == 0, 1 - me_x, me_x)
        acc = jnp.zeros((rows1, ob), F32)
        for a in range(3):
            for b in range(3):
                lhs = x3[b, m, a : a + side].reshape(rows1, cb)
                acc = acc + jnp.dot(lhs, wf[a, b], preferred_element_type=F32)
        t1[turn] = acc

    pl.semaphore_wait(barrier, 7 + jnp.where(me_z > 0, 1, 0) + jnp.where(me_z < zn - 1, 1, 0))

    p1s[...] = t1[0].astype(BF16)
    send1 = remote(p1s, p1r, p1_sem.at[0], p1_sem.at[1], me_i, 1 - me_x, me_z)
    send1.start()
    send1.wait_recv()
    line[me_z] = (res16[...].reshape(rows1, ob) + t1[1] + p1r[...].astype(F32)).astype(BF16)
    own_image = me_i * 2 + me_x

    def up(ref, slot, send, recv, kind):
        return remote(ref.at[slot], ref.at[slot], send.at[slot, kind], recv.at[slot], me_i, me_x, me_z + 1)

    def down(ref, slot, send, recv, kind):
        return remote(ref.at[slot], ref.at[slot], send.at[slot, kind], recv.at[slot], me_i, me_x, me_z - 1)

    def seg_send(source, other):
        cin = 1 - me_x if other else me_x
        return remote(
            line.at[source],
            segr.at[own_image],
            line_send.at[source, 2 + other],
            seg_recv.at[own_image],
            source,
            cin,
            me_z,
        )

    def line_copies(source, act):
        goes_up = jnp.logical_and(source <= me_z, me_z < zn - 1)
        goes_down = jnp.logical_and(source >= me_z, me_z > 0)

        @pl.when(goes_up)
        def _():
            act(up(line, source, line_send, line_recv, 0))

        @pl.when(goes_down)
        def _():
            act(down(line, source, line_send, line_recv, 1))

        act(seg_send(source, 1))

        @pl.when(source != me_i)
        def _():
            act(seg_send(source, 0))

    for rank in range(zn):
        source = by_distance(me_z, zn, rank)
        if rank:
            up(line, source, line_send, line_recv, 0).wait_recv()
        line_copies(source, lambda copy: copy.start())

    segr[own_image] = line[me_i]

    @pl.loop(0, 8)
    def _(image):
        @pl.when(image != own_image)
        def _():
            remote(
                line.at[0], segr.at[image], line_send.at[0, 2], seg_recv.at[image], me_i, 1 - me_x, me_z
            ).wait_recv()

    @pl.loop(0, side)
    def _(prow):
        for image in range(8):
            value = segr[image, pl.ds(pl.multiple_of(prow * q16, q16), q16), :].astype(F32)
            value = jnp.maximum(value, 0.0)
            for ct in range(ob // 128):
                s2[ct, pl.ds(((prow + 1) * 16 + 1) * 8 + image, side, stride=8), :] = value[
                    0:side, ct * 128 : ct * 128 + 128
                ]

    @pl.loop(0, 3)
    def _(a):
        for b in range(3):
            for ct in range(ob // 128):
                parts = []
                for p in range(half):
                    for q in range(half):
                        start = (2 * p * 16 + 2 * q + b) * 8 + a * 128
                        parts.append(s2[ct, pl.ds(pl.multiple_of(start, 8), 8), :])
                parts.append(jnp.zeros((8, 128), F32))
                column = a * (3 * ob) + b * ob + ct * 128
                x9[:, pl.ds(pl.multiple_of(column, 128), 128)] = jnp.concatenate(parts, axis=0).astype(BF16)

    load_wr.wait()

    def core_copy(yy):
        return remote(cs.at[yy], rc.at[yy], core_send.at[yy], core_recv.at[yy], core_peer, me_x, me_z)

    @pl.loop(0, 4)
    def _(item):
        yy = jnp.where(lax.rem(item, 2) == 0, 1 - me_y, me_y)
        cc = jnp.where(item < 2, 1 - core, core)
        column = pl.multiple_of((yy * 2 + cc) * kb, kb)
        weights = wr[:, :, :, pl.ds(column, kb)].reshape(9 * ob, kb)
        value = jnp.dot(x9[...], weights, preferred_element_type=F32)

        @pl.when(item < 2)
        def _():
            cs[yy] = value.astype(BF16)
            core_copy(yy).start()

        @pl.when(item >= 2)
        def _():
            p2[item - 2] = value

    core_copy(1 - me_y).wait_recv()
    ys[...] = (p2[0] + rc[1 - me_y].astype(F32)).astype(BF16)
    y_copy = remote(ys, ry, y_sem.at[0], y_sem.at[1], y_peer, me_x, me_z)
    y_copy.start()
    core_copy(me_y).wait_recv()
    own_sum = p2[1] + rc[me_y].astype(F32)
    p2[1] = own_sum
    y_copy.wait_recv()
    nar[me_z * 4 + me_i] = jnp.maximum(p2[1] + ry[...].astype(F32), 0.0).astype(BF16)

    @pl.loop(0, ww.shape[0])
    def _(chunk):
        load_ww(chunk).wait()

    def to_core(slot):
        return remote(nar.at[slot], nar.at[slot], nar_send.at[slot, 2], nar_recv.at[slot], core_peer, me_x, me_z)

    def to_y(slot):
        return remote(nar.at[slot], nar.at[slot], nar_send.at[slot, 3], nar_recv.at[slot], y_peer, me_x, me_z)

    def nar_copies(source, act):
        slot = source * 4 + me_i
        goes_up = jnp.logical_and(source <= me_z, me_z < zn - 1)
        goes_down = jnp.logical_and(source >= me_z, me_z > 0)

        @pl.when(goes_up)
        def _():
            act(up(nar, slot, nar_send, nar_recv, 0))

        @pl.when(goes_down)
        def _():
            act(down(nar, slot, nar_send, nar_recv, 1))

        act(to_y(slot))
        act(to_core(slot))

    def ranked(rank):
        value = 0
        for k in range(zn):
            value = value + jnp.where(rank == k, by_distance(me_z, zn, k), 0)
        return value

    @pl.loop(0, zn + 1)
    def _(rank):
        now = ranked(rank)
        before = ranked(rank - 1)

        @pl.when(rank < zn)
        def _():
            @pl.when(rank > 0)
            def _():
                to_core(now * 4 + me_i).wait_recv()

            nar_copies(now, lambda copy: copy.start())

        @pl.when(rank > 0)
        def _():
            slot = before * 4 + y_peer
            to_core(slot).wait_recv()
            to_core(slot).start()

        @pl.loop(0, 4)
        def _(part):
            late = part >= 2
            source = jnp.where(late, before, now)
            row = jnp.where(late, 1 - me_y, me_y)
            across = lax.rem(part, 2)
            slot = source * 4 + row * 2 + jnp.where(across == 1, 1 - core, core)

            @pl.when(jnp.where(late, rank > 0, rank < zn))
            def _():
                @pl.when(across == 1)
                def _():
                    to_core(slot).wait_recv()

                npad[1 : 1 + half, 1 : 1 + half] = (
                    nar[slot].astype(F32)[0:rows].reshape(half, half, 8, kb)
                )
                for a in range(3):
                    for b in range(3):
                        value = npad[a : a + half, b : b + half].reshape(rows, kb)
                        value = jnp.concatenate([value, jnp.zeros((8, kb), F32)], axis=0)
                        x9[:, (a * 3 + b) * kb : (a * 3 + b + 1) * kb] = value.astype(BF16)
                for n in range(0, total.shape[1], 256):
                    weights = ww[slot, :, :, :, n : n + 256].reshape(9 * kb, 256)
                    total[0 : rows + 8, n : n + 256] += jnp.dot(x9[...], weights, preferred_element_type=F32)

    pairs = total[...].reshape(total.shape[0] // 16, 16, total.shape[1])
    even, odd = pairs[:, 0:8], pairs[:, 8:16]
    first = lax.broadcasted_iota(jnp.int32, even.shape, 1) < 4
    low = jnp.where(first, even, pltpu.roll(odd, 4, 1)).reshape(-1, total.shape[1])
    high = jnp.where(first, pltpu.roll(even, 4, 1), odd).reshape(-1, total.shape[1])
    fs[...] = jnp.where(me_x == 0, high, low).astype(BF16)
    last = remote(fs, fr, f_sem.at[0], f_sem.at[1], me_i, 1 - me_x, me_z)
    last.start()
    mine = jnp.where(me_x == 0, low, high)
    last.wait_recv()
    out[...] = (mine + fr[...].astype(F32)).astype(BF16)

    send1.wait_send()
    for rank in range(zn):
        source = by_distance(me_z, zn, rank)
        line_copies(source, lambda copy: copy.wait_send())
        nar_copies(source, lambda copy: copy.wait_send())
        to_core(source * 4 + y_peer).wait_send()
    core_copy(0).wait_send()
    core_copy(1).wait_send()
    y_copy.wait_send()
    last.wait_send()


def fused(dims, maps, w_first, w_reduce, w_wide):
    side, half = maps.shape[2], maps.shape[2] // 2
    cb, ob = w_first.shape[2], w_first.shape[3]
    zn = dims["cout"]
    kb = w_reduce.shape[3] // dims["img"]
    width = w_wide.shape[3]
    chunks = w_wide.shape[2] // kb
    q16 = -(-side // 16) * 16
    rows1 = side * q16
    npos = half * half
    rows = npos * 8 + 8
    final = -(-npos // 4) * 4 * 8
    dma = pltpu.SemaphoreType.DMA
    vmem = pltpu.VMEM
    scratch = [
        vmem(w_first.shape, BF16),
        vmem(w_reduce.shape, BF16),
        vmem((chunks, 3, 3, kb, width), BF16),
        vmem((2, side, side, cb), BF16),
        vmem((side, side, ob), BF16),
        vmem((side, q16 + 16, cb), F32),
        vmem((3, 2, side + 2, q16, cb), BF16),
        vmem((2, rows1, ob), F32),
        vmem((side, q16, ob), F32),
        vmem((rows1, ob), BF16),
        vmem((rows1, ob), BF16),
        vmem((zn, rows1, ob), BF16),
        vmem((8, rows1, ob), BF16),
        vmem((ob // 128, (side + 2) * 16 * 8, 128), F32),
        vmem((rows, 9 * kb), BF16),
        vmem((2, rows, kb), F32),
        vmem((2, rows, kb), BF16),
        vmem((2, rows, kb), BF16),
        vmem((rows, kb), BF16),
        vmem((rows, kb), BF16),
        vmem((chunks, rows, kb), BF16),
        vmem((half + 2, half + 2, 8, kb), F32),
        vmem((final, width), F32),
        vmem((final // 2, width), BF16),
        vmem((final // 2, width), BF16),
        dma((4,)),
        dma((chunks,)),
        dma((2,)),
        dma((zn, 4)),
        dma((zn,)),
        dma((8,)),
        dma((2,)),
        dma((2,)),
        dma((2,)),
        dma((chunks, 4)),
        dma((chunks,)),
        dma((2,)),
    ]
    flops = 2 * 9 * (2 * side * side * cb * ob + npos * 8 * (ob * 4 * kb + chunks * kb * width))
    value = pl.pallas_call(
        functools.partial(segment_kernel, dict(dims, side=side, half=half)),
        out_shape=jax.ShapeDtypeStruct((final // 2, width), BF16),
        in_specs=[pl.BlockSpec(memory_space=pl.ANY)] * 4,
        out_specs=pl.BlockSpec(memory_space=vmem),
        scratch_shapes=scratch,
        compiler_params=pltpu.CompilerParams(
            collective_id=0, has_side_effects=True, vmem_limit_bytes=63 * 1024 * 1024
        ),
        cost_estimate=pl.CostEstimate(
            flops=flops, bytes_accessed=2 * (w_first.size + w_reduce.size + w_wide.size), transcendentals=0
        ),
    )(maps, w_first, w_reduce, w_wide)
    value = value[: npos * 4].reshape(half, half, 2, 2, width)
    return value.transpose(3, 2, 0, 1, 4)


def conv_block(padded, weight_flat, size, step):
    channels = padded.shape[3]
    windows = []
    for row_tap in range(3):
        for col_tap in range(3):
            windows.append(
                padded[
                    :,
                    row_tap : row_tap + step * (size - 1) + 1 : step,
                    col_tap : col_tap + step * (size - 1) + 1 : step,
                    :,
                ]
            )
    table = jnp.concatenate(windows, axis=3).reshape(-1, 9 * channels)
    total = jnp.dot(table, weight_flat, preferred_element_type=jnp.float32)
    return total.reshape(padded.shape[0], size, size, weight_flat.shape[1])


def conv_taps(padded, weight, size, step):
    count = padded.shape[0]
    channels = padded.shape[3]
    weight_flat = weight.reshape(9 * channels, weight.shape[3])
    group = 1
    for trial in range(1, 9):
        if count % trial == 0:
            group = trial
    blocks = padded.reshape(count // group, group, padded.shape[1], padded.shape[2], channels)
    results = lax.map(lambda block: conv_block(block, weight_flat, size, step), blocks)
    return results.reshape(count, size, size, weight.shape[3])


def pad_map(values):
    return jnp.pad(values, ((0, 0), (1, 1), (1, 1), (0, 0)))


def plain(maps, w_first, w_reduce, w_wide):
    batches = maps.shape[0]
    side = maps.shape[2]
    half = side // 2
    in_block = w_first.shape[2]
    out_block = w_first.shape[3]
    flat = maps.reshape(-1, side, side, maps.shape[4])
    in_part = lax.dynamic_slice_in_dim(flat, lax.axis_index("cin") * in_block, in_block, 3)
    first_terms = conv_taps(pad_map(jnp.maximum(in_part, 0)), w_first, side, 1)
    first_terms = first_terms.reshape(batches, maps.shape[1], side, side, out_block)
    summed = lax.psum(first_terms, "cin")
    own_part = lax.dynamic_slice_in_dim(maps, lax.axis_index("cout") * out_block, out_block, 4)
    segment_maps = (own_part.astype(jnp.float32) + summed).astype(jnp.bfloat16)
    whole = lax.all_gather(segment_maps, "cout", axis=4, tiled=True)
    by_channel = lax.all_to_all(whole, "img", split_axis=4, concat_axis=1, tiled=True)
    images = by_channel.shape[1]
    rect_segment = jnp.maximum(by_channel, 0).reshape(-1, side, side, by_channel.shape[4])
    reduced = conv_taps(pad_map(rect_segment), w_reduce, half, 2).reshape(
        batches, images, half, half, w_reduce.shape[3]
    )
    out_width = w_wide.shape[3]
    share = lax.psum_scatter(reduced, "img", scatter_dimension=1, tiled=True)
    narrow = jnp.maximum(share, 0.0).astype(jnp.bfloat16)
    gathered = lax.all_gather(narrow, "cout", axis=4, tiled=True)
    piece = lax.all_gather(gathered, "img", axis=1, tiled=True)
    count = piece.shape[1]
    flat_piece = piece.reshape(-1, half, half, piece.shape[4])
    partial_value = conv_taps(pad_map(flat_piece), w_wide, half, 1).reshape(
        batches, count, half, half, out_width
    )
    result = lax.psum_scatter(
        partial_value.astype(jnp.bfloat16), "cin", scatter_dimension=1, tiled=True
    )
    return result


def fits(dims, maps, w_first, w_reduce, w_wide):
    side = maps.shape[2]
    kb = w_reduce.shape[3] // dims["img"]
    return (
        dims["img"] == 4
        and dims["cout"] == 4
        and dims["cin"] == 2
        and maps.shape[0] == 2
        and maps.shape[1] == 1
        and side % 2 == 0
        and side <= 14
        and w_first.shape[2] % 128 == 0
        and w_first.shape[3] % 128 == 0
        and w_reduce.shape[2] == w_first.shape[3] == kb
        and w_wide.shape[2] == 16 * kb
        and w_wide.shape[3] % 256 == 0
    )


def solution(mesh):
    in_specs = (
        P(None, "img", None, None, None),
        P(None, None, "cin", "cout"),
        P(None, None, "img", ("cin", "cout")),
        P(None, None, "cin", ("img", "cout")),
    )
    out_specs = P(None, "cin", None, None, ("img", "cout"))
    dims = dict(mesh.shape)

    def local(*arrays):
        if fits(dims, *arrays):
            return fused(dims, *arrays)
        return plain(*arrays)

    return jax.shard_map(local, mesh=mesh, in_specs=in_specs, out_specs=out_specs, check_vma=False)
```

```python
import functools

import jax
import jax.numpy as jnp
from jax import lax
from jax.experimental import pallas as pl
from jax.experimental.pallas import tpu as pltpu
from jax.sharding import PartitionSpec as P

MESH = pl.DeviceIdType.MESH
F32 = jnp.float32
BF16 = jnp.bfloat16


def by_distance(position, count, rank):
    value = 0
    for place in range(count):
        order = sorted(range(count), key=lambda other: (abs(other - place), other))
        value = value + jnp.where(position == place, order[rank], 0)
    return value


def segment_kernel(
    dims,
    maps,
    w_first,
    w_reduce,
    w_wide,
    out,
    wf,
    wr,
    ww,
    xin,
    resid,
    xpad,
    x3,
    t1,
    res16,
    p1s,
    p1r,
    line,
    segr,
    s2,
    x9,
    p2,
    cs,
    rc,
    ys,
    ry,
    nar,
    npad,
    total,
    fs,
    fr,
    load_sem,
    ww_sem,
    p1_sem,
    line_send,
    line_recv,
    seg_recv,
    core_send,
    core_recv,
    y_sem,
    nar_send,
    nar_recv,
    f_sem,
):
    zn = dims["cout"]
    side, half = dims["side"], dims["half"]
    me_i, me_x, me_z = lax.axis_index("img"), lax.axis_index("cin"), lax.axis_index("cout")
    core, me_y = lax.rem(me_i, 2), me_i // 2
    core_peer = me_y * 2 + (1 - core)
    y_peer = (1 - me_y) * 2 + core
    cb = wf.shape[2]
    ob = wf.shape[3]
    q16 = x3.shape[3]
    rows1 = side * q16
    kb = ry.shape[0] * ry.shape[2]
    npos = half * half
    rows = npos * 8

    def remote(src, dst, send, recv, img, cin, cout):
        return pltpu.make_async_remote_copy(
            src_ref=src,
            dst_ref=dst,
            send_sem=send,
            recv_sem=recv,
            device_id=(img, cin, cout),
            device_id_type=MESH,
        )

    load_wf = pltpu.make_async_copy(w_first, wf, load_sem.at[0])
    load_x = pltpu.make_async_copy(
        maps.at[:, 0, :, :, pl.ds(pl.multiple_of(me_x * cb, cb), cb)], xin, load_sem.at[1]
    )
    load_r = pltpu.make_async_copy(
        maps.at[me_x, 0, :, :, pl.ds(pl.multiple_of(me_z * ob, ob), ob)], resid, load_sem.at[2]
    )
    load_wr = pltpu.make_async_copy(w_reduce, wr, load_sem.at[3])
    load_x.start()
    load_wf.start()
    load_r.start()
    load_wr.start()

    def load_ww(chunk):
        return pltpu.make_async_copy(
            w_wide.at[:, :, pl.ds(pl.multiple_of(chunk * kb, kb), kb), :], ww.at[chunk], ww_sem.at[chunk]
        )

    @pl.loop(0, ww.shape[0])
    def _(chunk):
        load_ww(chunk).start()

    barrier = pltpu.get_barrier_semaphore()
    for di in range(4):
        for dx in range(2):
            if di or dx:
                pl.semaphore_signal(
                    barrier,
                    inc=1,
                    device_id=(lax.rem(me_i + di, 4), lax.rem(me_x + dx, 2), me_z),
                    device_id_type=MESH,
                )

    @pl.when(me_z > 0)
    def _():
        pl.semaphore_signal(barrier, inc=1, device_id=(me_i, me_x, me_z - 1), device_id_type=MESH)

    @pl.when(me_z < zn - 1)
    def _():
        pl.semaphore_signal(barrier, inc=1, device_id=(me_i, me_x, me_z + 1), device_id_type=MESH)

    xpad[...] = jnp.zeros_like(xpad)
    x3[...] = jnp.zeros_like(x3)
    res16[...] = jnp.zeros_like(res16)
    load_x.wait()
    for m in range(2):
        xpad[:, 8 : 8 + side, :] = jnp.maximum(xin[m].astype(F32), 0.0)
        for b in range(3):
            x3[b, m, 1 : 1 + side] = xpad[:, 7 + b : 7 + b + q16, :].astype(BF16)
    load_r.wait()
    res16[:, 0:side, :] = resid[...].astype(F32)
    load_wf.wait()

    @pl.loop(0, 2)
    def _(turn):
        m = jnp.where(turn == 0, 1 - me_x, me_x)
        acc = jnp.zeros((rows1, ob), F32)
        for a in range(3):
            for b in range(3):
                lhs = x3[b, m, a : a + side].reshape(rows1, cb)
                acc = acc + jnp.dot(lhs, wf[a, b], preferred_element_type=F32)
        t1[turn] = acc

    pl.semaphore_wait(barrier, 7 + jnp.where(me_z > 0, 1, 0) + jnp.where(me_z < zn - 1, 1, 0))

    part1 = rows1 // 2

    def p1_copy(h):
        return remote(p1s.at[h], p1r.at[h], p1_sem.at[h, 0], p1_sem.at[h, 1], me_i, 1 - me_x, me_z)

    for h in range(2):
        p1s[h] = t1[0, h * part1 : (h + 1) * part1].astype(BF16)
        p1_copy(h).start()
    s2[...] = jnp.zeros_like(s2)
    npad[...] = jnp.zeros_like(npad)
    total[...] = jnp.zeros_like(total)
    own_image = me_i * 2 + me_x

    def along(ref, slot, h, send, recv, kind):
        place = ref.at[slot, h]
        target = me_z + 1 if kind == 0 else me_z - 1
        return remote(place, place, send.at[slot, h, kind], recv.at[slot, h], me_i, me_x, target)

    def seg_send(source, h, other):
        cin = 1 - me_x if other else me_x
        return remote(
            line.at[source, h],
            segr.at[own_image, h],
            line_send.at[source, h, 2 + other],
            seg_recv.at[own_image, h],
            source,
            cin,
            me_z,
        )

    def line_copies(source, h, act):
        goes_up = jnp.logical_and(source <= me_z, me_z < zn - 1)
        goes_down = jnp.logical_and(source >= me_z, me_z > 0)

        @pl.when(goes_up)
        def _():
            act(along(line, source, h, line_send, line_recv, 0))

        @pl.when(goes_down)
        def _():
            act(along(line, source, h, line_send, line_recv, 1))

        act(seg_send(source, h, 1))

        @pl.when(source != me_i)
        def _():
            act(seg_send(source, h, 0))

    for h in range(2):
        p1_copy(h).wait_recv()
        kept = res16[h * (side // 2) : (h + 1) * (side // 2)].reshape(part1, ob)
        mine1 = t1[1, h * part1 : (h + 1) * part1]
        line[me_z, h] = (kept + mine1 + p1r[h].astype(F32)).astype(BF16)
        line_copies(me_z, h, lambda copy: copy.start())
    for rank in range(1, zn):
        source = by_distance(me_z, zn, rank)
        for h in range(2):
            along(line, source, h, line_send, line_recv, 0).wait_recv()
            line_copies(source, h, lambda copy: copy.start())

    segr[own_image] = line[me_i]

    @pl.loop(0, 8)
    def _(image):
        @pl.when(image != own_image)
        def _():
            for h in range(2):
                remote(
                    line.at[0, h],
                    segr.at[image, h],
                    line_send.at[0, h, 2],
                    seg_recv.at[image, h],
                    me_i,
                    1 - me_x,
                    me_z,
                ).wait_recv()

    @pl.loop(0, side)
    def _(prow):
        for image in range(8):
            within = pl.multiple_of(lax.rem(prow, side // 2) * q16, q16)
            value = segr[image, prow // (side // 2), pl.ds(within, q16), :].astype(F32)
            value = jnp.maximum(value, 0.0)
            for ct in range(ob // 128):
                s2[ct, pl.ds(((prow + 1) * 16 + 1) * 8 + image, side, stride=8), :] = value[
                    0:side, ct * 128 : ct * 128 + 128
                ]

    @pl.loop(0, 3)
    def _(a):
        for b in range(3):
            for ct in range(ob // 128):
                parts = []
                for p in range(half):
                    for q in range(half):
                        start = (2 * p * 16 + 2 * q + b) * 8 + a * 128
                        parts.append(s2[ct, pl.ds(pl.multiple_of(start, 8), 8), :])
                parts.append(jnp.zeros((8, 128), F32))
                column = a * (3 * ob) + b * ob + ct * 128
                x9[:, pl.ds(pl.multiple_of(column, 128), 128)] = jnp.concatenate(parts, axis=0).astype(BF16)

    load_wr.wait()

    def core_copy(yy):
        return remote(cs.at[yy], rc.at[yy], core_send.at[yy], core_recv.at[yy], core_peer, me_x, me_z)

    hb = kb // 2

    def y_copy(h):
        return remote(ys.at[h], ry.at[h], y_sem.at[h, 0], y_sem.at[h, 1], y_peer, me_x, me_z)

    @pl.loop(0, 4)
    def _(item):
        yy = jnp.where(lax.rem(item, 2) == 0, 1 - me_y, me_y)
        cc = jnp.where(item < 2, 1 - core, core)
        column = pl.multiple_of((yy * 2 + cc) * kb, kb)
        weights = wr[:, :, :, pl.ds(column, kb)].reshape(9 * ob, kb)
        value = jnp.dot(x9[...], weights, preferred_element_type=F32)

        @pl.when(item < 2)
        def _():
            cs[yy] = value.astype(BF16)
            core_copy(yy).start()

        @pl.when(item == 2)
        def _():
            core_copy(1 - me_y).wait_recv()
            far = value + rc[1 - me_y].astype(F32)
            for h in range(2):
                ys[h] = far[:, h * hb : (h + 1) * hb].astype(BF16)
                y_copy(h).start()

        @pl.when(item == 3)
        def _():
            p2[...] = value

    core_copy(me_y).wait_recv()
    p2[...] = p2[...] + rc[me_y].astype(F32)

    def to_core(slot, h):
        place = nar.at[slot, h]
        return remote(place, place, nar_send.at[slot, h, 2], nar_recv.at[slot, h], core_peer, me_x, me_z)

    def to_y(slot, h):
        place = nar.at[slot, h]
        return remote(place, place, nar_send.at[slot, h, 3], nar_recv.at[slot, h], y_peer, me_x, me_z)

    def nar_copies(source, h, act):
        slot = source * 4 + me_i
        goes_up = jnp.logical_and(source <= me_z, me_z < zn - 1)
        goes_down = jnp.logical_and(source >= me_z, me_z > 0)

        @pl.when(goes_up)
        def _():
            act(along(nar, slot, h, nar_send, nar_recv, 0))

        @pl.when(goes_down)
        def _():
            act(along(nar, slot, h, nar_send, nar_recv, 1))

        act(to_y(slot, h))
        act(to_core(slot, h))

    for h in range(2):
        y_copy(h).wait_recv()
        own_sum = p2[:, h * hb : (h + 1) * hb] + ry[h].astype(F32)
        nar[me_z * 4 + me_i, h] = jnp.maximum(own_sum, 0.0).astype(BF16)
        nar_copies(me_z, h, lambda copy: copy.start())

    @pl.loop(0, ww.shape[0])
    def _(chunk):
        load_ww(chunk).wait()

    def ranked(rank):
        value = 0
        for k in range(zn):
            value = value + jnp.where(rank == k, by_distance(me_z, zn, k), 0)
        return value

    @pl.loop(0, zn + 1)
    def _(rank):
        now = ranked(rank)
        before = ranked(rank - 1)

        for h in range(2):

            @pl.when(jnp.logical_and(rank > 0, rank < zn))
            def _():
                to_core(now * 4 + me_i, h).wait_recv()
                nar_copies(now, h, lambda copy: copy.start())

            @pl.when(rank > 0)
            def _():
                slot = before * 4 + y_peer
                to_core(slot, h).wait_recv()
                to_core(slot, h).start()

        @pl.loop(0, 4)
        def _(part):
            late = part >= 2
            source = jnp.where(late, before, now)
            row = jnp.where(late, 1 - me_y, me_y)
            across = lax.rem(part, 2)
            slot = source * 4 + row * 2 + jnp.where(across == 1, 1 - core, core)

            @pl.when(jnp.where(late, rank > 0, rank < zn))
            def _():
                @pl.when(across == 1)
                def _():
                    to_core(slot, 0).wait_recv()
                    to_core(slot, 1).wait_recv()

                for h in range(2):
                    npad[1 : 1 + half, 1 : 1 + half, :, h * hb : (h + 1) * hb] = (
                        nar[slot, h].astype(F32)[0:rows].reshape(half, half, 8, hb)
                    )
                for a in range(3):
                    for b in range(3):
                        value = npad[a : a + half, b : b + half].reshape(rows, kb)
                        value = jnp.concatenate([value, jnp.zeros((8, kb), F32)], axis=0)
                        x9[:, (a * 3 + b) * kb : (a * 3 + b + 1) * kb] = value.astype(BF16)
                for n in range(0, total.shape[1], 256):
                    weights = ww[slot, :, :, :, n : n + 256].reshape(9 * kb, 256)
                    total[0 : rows + 8, n : n + 256] += jnp.dot(x9[...], weights, preferred_element_type=F32)

    pairs = total[...].reshape(total.shape[0] // 16, 16, total.shape[1])
    even, odd = pairs[:, 0:8], pairs[:, 8:16]
    first = lax.broadcasted_iota(jnp.int32, even.shape, 1) < 4
    low = jnp.where(first, even, pltpu.roll(odd, 4, 1)).reshape(-1, total.shape[1])
    high = jnp.where(first, pltpu.roll(even, 4, 1), odd).reshape(-1, total.shape[1])
    fs[...] = jnp.where(me_x == 0, high, low).astype(BF16)
    last = remote(fs, fr, f_sem.at[0], f_sem.at[1], me_i, 1 - me_x, me_z)
    last.start()
    mine = jnp.where(me_x == 0, low, high)
    last.wait_recv()
    out[...] = (mine + fr[...].astype(F32))[0 : out.shape[0]].astype(BF16)

    for h in range(2):
        p1_copy(h).wait_send()
        y_copy(h).wait_send()
        core_copy(h).wait_send()
        for rank in range(zn):
            source = by_distance(me_z, zn, rank)
            line_copies(source, h, lambda copy: copy.wait_send())
            nar_copies(source, h, lambda copy: copy.wait_send())
            to_core(source * 4 + y_peer, h).wait_send()
    last.wait_send()


def fused(dims, maps, w_first, w_reduce, w_wide):
    side, half = maps.shape[2], maps.shape[2] // 2
    cb, ob = w_first.shape[2], w_first.shape[3]
    zn = dims["cout"]
    kb = w_reduce.shape[3] // dims["img"]
    width = w_wide.shape[3]
    chunks = w_wide.shape[2] // kb
    q16 = -(-side // 16) * 16
    rows1 = side * q16
    npos = half * half
    rows = npos * 8 + 8
    final = -(-npos // 4) * 4 * 8
    dma = pltpu.SemaphoreType.DMA
    vmem = pltpu.VMEM
    scratch = [
        vmem(w_first.shape, BF16),
        vmem(w_reduce.shape, BF16),
        vmem((chunks, 3, 3, kb, width), BF16),
        vmem((2, side, side, cb), BF16),
        vmem((side, side, ob), BF16),
        vmem((side, q16 + 16, cb), F32),
        vmem((3, 2, side + 2, q16, cb), BF16),
        vmem((2, rows1, ob), F32),
        vmem((side, q16, ob), F32),
        vmem((2, rows1 // 2, ob), BF16),
        vmem((2, rows1 // 2, ob), BF16),
        vmem((zn, 2, rows1 // 2, ob), BF16),
        vmem((8, 2, rows1 // 2, ob), BF16),
        vmem((ob // 128, (side + 2) * 16 * 8, 128), F32),
        vmem((rows, 9 * kb), BF16),
        vmem((rows, kb), F32),
        vmem((2, rows, kb), BF16),
        vmem((2, rows, kb), BF16),
        vmem((2, rows, kb // 2), BF16),
        vmem((2, rows, kb // 2), BF16),
        vmem((chunks, 2, rows, kb // 2), BF16),
        vmem((half + 2, half + 2, 8, kb), F32),
        vmem((final, width), F32),
        vmem((final // 2, width), BF16),
        vmem((final // 2, width), BF16),
        dma((4,)),
        dma((chunks,)),
        dma((2, 2)),
        dma((zn, 2, 4)),
        dma((zn, 2)),
        dma((8, 2)),
        dma((2,)),
        dma((2,)),
        dma((2, 2)),
        dma((chunks, 2, 4)),
        dma((chunks, 2)),
        dma((2,)),
    ]
    flops = 2 * 9 * (2 * side * side * cb * ob + npos * 8 * (ob * 4 * kb + chunks * kb * width))
    value = pl.pallas_call(
        functools.partial(segment_kernel, dict(dims, side=side, half=half)),
        out_shape=jax.ShapeDtypeStruct((npos * 4, width), BF16),
        in_specs=[pl.BlockSpec(memory_space=pl.ANY)] * 4,
        out_specs=pl.BlockSpec(memory_space=vmem),
        scratch_shapes=scratch,
        compiler_params=pltpu.CompilerParams(
            collective_id=0, has_side_effects=True, vmem_limit_bytes=63 * 1024 * 1024
        ),
        cost_estimate=pl.CostEstimate(
            flops=flops, bytes_accessed=2 * (w_first.size + w_reduce.size + w_wide.size), transcendentals=0
        ),
    )(maps, w_first, w_reduce, w_wide)
    value = value.reshape(half, half, 2, 2, width)
    return value.transpose(3, 2, 0, 1, 4)


def conv_block(padded, weight_flat, size, step):
    channels = padded.shape[3]
    windows = []
    for row_tap in range(3):
        for col_tap in range(3):
            windows.append(
                padded[
                    :,
                    row_tap : row_tap + step * (size - 1) + 1 : step,
                    col_tap : col_tap + step * (size - 1) + 1 : step,
                    :,
                ]
            )
    table = jnp.concatenate(windows, axis=3).reshape(-1, 9 * channels)
    total = jnp.dot(table, weight_flat, preferred_element_type=jnp.float32)
    return total.reshape(padded.shape[0], size, size, weight_flat.shape[1])


def conv_taps(padded, weight, size, step):
    count = padded.shape[0]
    channels = padded.shape[3]
    weight_flat = weight.reshape(9 * channels, weight.shape[3])
    group = 1
    for trial in range(1, 9):
        if count % trial == 0:
            group = trial
    blocks = padded.reshape(count // group, group, padded.shape[1], padded.shape[2], channels)
    results = lax.map(lambda block: conv_block(block, weight_flat, size, step), blocks)
    return results.reshape(count, size, size, weight.shape[3])


def pad_map(values):
    return jnp.pad(values, ((0, 0), (1, 1), (1, 1), (0, 0)))


def plain(maps, w_first, w_reduce, w_wide):
    batches = maps.shape[0]
    side = maps.shape[2]
    half = side // 2
    in_block = w_first.shape[2]
    out_block = w_first.shape[3]
    flat = maps.reshape(-1, side, side, maps.shape[4])
    in_part = lax.dynamic_slice_in_dim(flat, lax.axis_index("cin") * in_block, in_block, 3)
    first_terms = conv_taps(pad_map(jnp.maximum(in_part, 0)), w_first, side, 1)
    first_terms = first_terms.reshape(batches, maps.shape[1], side, side, out_block)
    summed = lax.psum(first_terms, "cin")
    own_part = lax.dynamic_slice_in_dim(maps, lax.axis_index("cout") * out_block, out_block, 4)
    segment_maps = (own_part.astype(jnp.float32) + summed).astype(jnp.bfloat16)
    whole = lax.all_gather(segment_maps, "cout", axis=4, tiled=True)
    by_channel = lax.all_to_all(whole, "img", split_axis=4, concat_axis=1, tiled=True)
    images = by_channel.shape[1]
    rect_segment = jnp.maximum(by_channel, 0).reshape(-1, side, side, by_channel.shape[4])
    reduced = conv_taps(pad_map(rect_segment), w_reduce, half, 2).reshape(
        batches, images, half, half, w_reduce.shape[3]
    )
    out_width = w_wide.shape[3]
    share = lax.psum_scatter(reduced, "img", scatter_dimension=1, tiled=True)
    narrow = jnp.maximum(share, 0.0).astype(jnp.bfloat16)
    gathered = lax.all_gather(narrow, "cout", axis=4, tiled=True)
    piece = lax.all_gather(gathered, "img", axis=1, tiled=True)
    count = piece.shape[1]
    flat_piece = piece.reshape(-1, half, half, piece.shape[4])
    partial_value = conv_taps(pad_map(flat_piece), w_wide, half, 1).reshape(
        batches, count, half, half, out_width
    )
    result = lax.psum_scatter(
        partial_value.astype(jnp.bfloat16), "cin", scatter_dimension=1, tiled=True
    )
    return result


def fits(dims, maps, w_first, w_reduce, w_wide):
    side = maps.shape[2]
    kb = w_reduce.shape[3] // dims["img"]
    return (
        dims["img"] == 4
        and dims["cout"] == 4
        and dims["cin"] == 2
        and maps.shape[0] == 2
        and maps.shape[1] == 1
        and side % 2 == 0
        and side <= 14
        and w_first.shape[2] % 128 == 0
        and w_first.shape[3] % 128 == 0
        and w_reduce.shape[2] == w_first.shape[3] == kb
        and kb % 256 == 0
        and w_wide.shape[2] == 16 * kb
        and w_wide.shape[3] % 256 == 0
    )


def solution(mesh):
    in_specs = (
        P(None, "img", None, None, None),
        P(None, None, "cin", "cout"),
        P(None, None, "img", ("cin", "cout")),
        P(None, None, "cin", ("img", "cout")),
    )
    out_specs = P(None, "cin", None, None, ("img", "cout"))
    dims = dict(mesh.shape)

    def local(*arrays):
        if fits(dims, *arrays):
            return fused(dims, *arrays)
        return plain(*arrays)

    return jax.shard_map(local, mesh=mesh, in_specs=in_specs, out_specs=out_specs, check_vma=False)
```
